512 devices in a mesh: layer: 16 (over x_lo, z), feat: 32 (over x_hi, y, core).
Axes of the slice: x: 4 (x_hi: 2, x_lo: 2; x = x_hi * 2 + x_lo), y: 8, z: 8, core: 2. Of those that a mesh axis runs over, the one named last changes fastest.
Arguments:
- grads: bfloat16 [2, 16, 256, 8192], P(None, 'layer', 'feat'), may hold values from -6 to 6
- decoder: bfloat16 [2, 16, 3072, 8192], P(None, 'layer', 'feat'), may hold values from -0.01171875 to 0.01171875
- active_ids: int32 [256, 128], replicated, may hold values from 0 to 3071, all different within a row
- act_vals: float32 [256, 128], P('layer'), may hold values from 0.2 to 2
Outputs:
- edges: float32 [256, 128], P('layer')
The draws below stay inside these ranges and needn't reach their ends.
Inputs may be any that keep to these rules, and one draw needn't show every extreme that they name: `active_ids`: each row names 128 different features; every feature is named by some row; a few features are named far more often than others.
All inputs are finite; a program needn't handle non-finite values.
Results may differ from the reference program's by a relative error of at most 0.0003.
Values may be sent and summed in bfloat16 or wider, within the bound.
A program may use at most 64 MiB of HBM per device.

```python
import math
import jax
import jax.numpy as jnp
from jax import lax

D = 8192
TOK = 256
ACT = 128
FEATS = 3072
N_LAYER = 16


def level_of(key, extent, shards, low, largest):
    gain = 1.0
    for dim, shards_of in shards:
        draws = jax.random.uniform(jax.random.fold_in(jax.random.fold_in(key, 6), dim), (shards_of,), jnp.float32, low / len(shards), largest / len(shards))
        gain = gain * jnp.repeat(jnp.exp(draws), extent[dim] // shards_of).reshape((-1,) + (1,) * (len(extent) - 1 - dim))
    return gain


def picks_of(rng, rows, count, top, lift):
    ranking = jax.random.permutation(jax.random.fold_in(rng, 1), count)
    pull = ranking
    for power in range(3):
        pull = pull * pull // count
    pull = pull * lift // count
    lots = jax.random.randint(jax.random.fold_in(rng, 2), (rows, count), 0, 4096) + pull
    holders = jax.random.permutation(jax.random.fold_in(rng, 3), rows)[jnp.arange(count) % rows]
    lots = jnp.where(jnp.arange(rows)[:, None] == holders[None, :], 1 << 14, lots)
    merit = lots * count + jnp.arange(count)
    return lax.top_k(merit.astype(jnp.int32), top)[1].astype(jnp.int32)


def scatter_about(own_key, extent, deviation, most, cuts=(), kind=jnp.bfloat16):
    drawn = deviation * jax.random.normal(own_key, extent, jnp.float32)
    if cuts:
        drawn = drawn * level_of(own_key, extent, cuts, -0.22, 0.18)
    return jnp.clip(drawn, -most, most).astype(kind)


def setup_inputs(seed: int = 0) -> dict:
    key_of = jax.random.split(jax.random.key(seed), 5)
    grads = scatter_about(key_of[0], (2, N_LAYER, TOK, D), 1.0, 6.0, ((1, 16), (2, 32)))
    decoder = scatter_about(key_of[1], (2, N_LAYER, FEATS, D), (D * 2 * N_LAYER) ** -0.5, 0.01171875, ((1, 16), (2, 32)))
    active_ids = picks_of(key_of[2], TOK, FEATS, ACT, 682)
    act_vals = jnp.clip(jnp.exp(math.log(2.0) - 2.3025851 * jax.random.uniform(key_of[3], (TOK, ACT), jnp.float32) ** level_of(key_of[3], (TOK, ACT), ((0, 16),), -0.2, 0.2)), 0.2, 2.0)
    return {"grads": grads, "decoder": decoder, "active_ids": active_ids, "act_vals": act_vals}


def reference(grads, decoder, active_ids, act_vals):
    pair_grads = grads.reshape((2 * N_LAYER, TOK, D))
    pair_decoder = decoder.reshape((2 * N_LAYER, FEATS, D))

    def accumulate(total, pieces):
        grad_layer, dec_layer = pieces
        return total + jnp.dot(grad_layer, dec_layer.T, preferred_element_type=jnp.float32), None

    start = jnp.zeros((TOK, FEATS), jnp.float32)
    scores, unused = lax.scan(accumulate, start, (pair_grads, pair_decoder))
    picked = jnp.take_along_axis(scores, active_ids.astype(jnp.int32), axis=1)
    return act_vals * picked
```

```python
import functools

import jax
import jax.numpy as jnp
from jax import lax
from jax.experimental import pallas as pl
from jax.experimental.pallas import tpu as pltpu
from jax.sharding import PartitionSpec as P

MESH = pl.DeviceIdType.MESH
F32 = jnp.float32

PARTS = {("A", 1): (0, 1792), ("A", 2): (1792, 1792), ("B", 1): (3584, 2304), ("B", 2): (5888, 2304)}
SPAN = {"A": (0, 3584), "B": (3584, 4608)}
RING = 8
CHIPS = 16
LAYERS = 16
N_SEND = 128
N_RECV = 112


def kernel(grads, dec, ids_hbm, act_hbm, out, got, feats, acc, ids, act, picked, r1, half_in, r2, halves,
           send_sem, recv_sem, r1_sem, r2_sem, loc_sem):
    layer = lax.axis_index("layer")
    feat = lax.axis_index("feat")
    core = lax.rem(feat, 2)
    chip = feat // 2
    row = lax.rem(chip, RING)
    side = chip // RING
    other = 1 - core
    rows = grads.shape[2]
    n_feats = dec.shape[2]

    def chip_at(which, off):
        base = side if which == 0 else 1 - side
        return base * RING + lax.rem(row + off + RING, RING)

    def same_core(which, off):
        return {"feat": chip_at(which, off) * 2 + core}

    sibling = {"feat": chip * 2 + other}
    partner = same_core(1, 0)

    local = [
        pltpu.make_async_copy(grads.at[core, 0], got.at[feat], loc_sem.at[0]),
        pltpu.make_async_copy(dec.at[core, 0], feats.at[core], loc_sem.at[1]),
        pltpu.make_async_copy(ids_hbm, ids, loc_sem.at[2]),
        pltpu.make_async_copy(act_hbm, act, loc_sem.at[3]),
    ]
    for copy in local:
        copy.start()

    barrier = pltpu.get_barrier_semaphore()
    peers = [sibling, partner, same_core(0, 1), same_core(0, -1)]
    peers += [{"layer": lax.rem(layer + r, LAYERS)} for r in range(1, LAYERS)]
    for peer in peers:
        pl.semaphore_signal(barrier, inc=1, device_id=peer, device_id_type=MESH)
    pl.semaphore_wait(barrier, len(peers))

    sends = []
    keys = {}

    def sem_of(key):
        return recv_sem.at[keys.setdefault(key, len(keys))]

    def send(src, dst, key, device):
        copy = pltpu.make_async_remote_copy(src, dst, send_sem.at[len(sends)], sem_of(key), device_id=device,
                                            device_id_type=MESH)
        copy.start()
        sends.append(copy)

    def arrive(dst, key):
        pltpu.make_async_remote_copy(dst, dst, send_sem.at[0], sem_of(key), device_id=sibling,
                                     device_id_type=MESH).wait_recv()

    def block(b, typ, part):
        lo, width = PARTS[typ, part]
        return got.at[pl.ds(2 * b, 2), :, pl.ds(lo, width)]

    for typ in ("B", "A"):
        lo, width = SPAN[typ]
        cols = pl.ds(lo, width)
        send(grads.at[other, 0, :, cols], got.at[feat, :, cols], ("swap", typ), sibling)

    def first(src, slot, typ):
        for part in (1, 2):
            lo, width = PARTS[typ, part]
            cols = pl.ds(lo, width)
            for s in (1, -1):
                send(src.at[:, cols], got.at[slot, :, cols], ("y", s, typ, 0, 0, part), same_core(0, s))

    def first_x(src, slot, typ):
        for part in (1, 2):
            lo, width = PARTS[typ, part]
            cols = pl.ds(lo, width)
            send(src.at[:, cols], got.at[slot, :, cols], ("x", typ, 0, part), partner)

    mine = grads.at[core, 0]
    first(mine, feat, "B")
    first_x(mine, feat, "A")
    sib_slot = chip * 2 + other
    sib_rows = got.at[sib_slot]
    for typ, xtyp in (("B", "A"), ("A", "B")):
        lo, width = SPAN[typ]
        if typ == "A":
            first(mine, feat, "A")
            first_x(mine, feat, "B")
            arrive(got.at[sib_slot, :, pl.ds(lo, width)], ("swap", typ))
            first(sib_rows, sib_slot, "A")
            first_x(sib_rows, sib_slot, "A")
            first_x(sib_rows, sib_slot, "B")
        else:
            arrive(got.at[sib_slot, :, pl.ds(lo, width)], ("swap", typ))
            first(sib_rows, sib_slot, "B")
    send(dec.at[other, 0], feats.at[core], ("dec",), sibling)

    def pass_on(typ, which, d):
        for part in (1, 2):
            for s in (1, -1):
                if d == 3 and (part == 1) != (s == 1):
                    continue
                off = -s * (d + 1)
                piece = block(chip_at(which, off), typ, part)
                arrive(piece, ("y", s, typ, which, d, part))
                if d < 2 or (d == 2 and (part == 1) == (s == 1)):
                    send(piece, piece, ("y", s, typ, which, d + 1, part), same_core(0, s))
                if typ == "B":
                    send(piece, piece, ("x", typ, off if d < 3 else 4, part), partner)

    def from_partner(typ, offs):
        for off in offs:
            for part in (1, 2):
                arrive(block(chip_at(1, off), typ, part), ("x", typ, off, part))

    def multiply(blocks, typ, new=False):
        lo, width = SPAN[typ]
        cols = pl.ds(lo, width)
        chips = [chip_at(which, off) for which, off in blocks]
        left = jnp.concatenate([got[pl.ds(2 * b, 2), :, cols].reshape(2 * rows, width) for b in chips], axis=0)
        right = feats[:, :, cols].reshape(2 * n_feats, width)
        part = lax.dot_general(left, right, (((1,), (1,)), ((), ())), preferred_element_type=F32)
        for k, b in enumerate(chips):
            term = part[2 * rows * k: 2 * rows * (k + 1)]
            if new:
                acc[b, :, pl.ds(0, 2 * n_feats)] = term
            else:
                acc[b, :, pl.ds(0, 2 * n_feats)] += term

    layer_sends = []

    def finish(blocks):
        for which, off in blocks:
            b = chip_at(which, off)
            here = ids[pl.ds(pl.multiple_of(2 * rows * b, 2 * rows), 2 * rows), :] - chip * (2 * n_feats)
            lanes = jnp.bitwise_and(here, 127)
            low = jnp.take_along_axis(acc[b, :, pl.ds(0, 128)], lanes, axis=1, mode="promise_in_bounds")
            high = jnp.take_along_axis(acc[b, :, pl.ds(128, 128)], lanes, axis=1, mode="promise_in_bounds")
            value = jnp.where(here < 128, low, high)
            inside = jnp.logical_and(here >= 0, here < 2 * n_feats)
            picked[b] = jnp.where(inside, value, F32(0.0))
            copy = pltpu.make_async_remote_copy(picked.at[b], r1.at[layer], send_sem.at[N_SEND - 1 - len(layer_sends)],
                                                r1_sem.at[layer], device_id={"layer": b}, device_id_type=MESH)
            layer_sends.append((b, copy))

            @pl.when(b != layer)
            def _():
                copy.start()

    acc[...] = jnp.zeros_like(acc)
    near = [(0, 0), (1, 0), (0, 1), (0, -1), (1, 1), (1, -1)]
    two = [(0, 2), (0, -2), (1, 2), (1, -2)]
    three = [(0, 3), (0, -3), (1, 3), (1, -3)]
    four = [(0, 4), (1, 4)]

    pass_on("B", 0, 0)
    for part in (1, 2):
        piece = block(chip_at(1, 0), "A", part)
        arrive(piece, ("x", "A", 0, part))
        for s in (1, -1):
            send(piece, piece, ("y", s, "A", 1, 0, part), same_core(0, s))
    pass_on("A", 0, 0)
    for copy in local:
        copy.wait()
    arrive(feats.at[other], ("dec",))
    pass_on("B", 0, 1)
    pass_on("A", 1, 0)
    multiply(near, "A", True)
    pass_on("A", 0, 1)
    from_partner("B", (0, 1, -1))
    multiply(near, "B")
    finish(near)
    pass_on("B", 0, 2)
    pass_on("A", 1, 1)
    multiply(two, "A", True)
    pass_on("B", 0, 3)
    from_partner("B", (2, -2))
    multiply(two, "B")
    finish(two)
    pass_on("A", 0, 2)
    pass_on("A", 1, 2)
    multiply(three, "A", True)
    from_partner("B", (3, -3))
    multiply(three, "B")
    finish(three)
    pass_on("A", 0, 3)
    pass_on("A", 1, 3)
    multiply(four, "A", True)
    from_partner("B", (4,))
    multiply(four, "B")
    finish(four)

    r1[layer] = picked[layer]
    for r in range(1, LAYERS):
        other_layer = lax.rem(layer + r, LAYERS)
        piece = r1.at[other_layer]
        pltpu.make_async_remote_copy(piece, piece, send_sem.at[0], r1_sem.at[other_layer], device_id=sibling,
                                     device_id_type=MESH).wait_recv()
    total = r1[0]
    for k in range(1, LAYERS):
        total += r1[k]
    halves[0] = total[:rows]
    halves[1] = total[rows:]
    send(halves.at[other], half_in, ("half",), sibling)
    arrive(half_in, ("half",))
    r2[chip] = halves[core] + half_in[...]
    chip_sends = []
    for r in range(1, CHIPS):
        to = lax.rem(chip + r, CHIPS)
        copy = pltpu.make_async_remote_copy(r2.at[chip], r2.at[chip], send_sem.at[N_SEND - 17 - r], r2_sem.at[chip],
                                            device_id={"feat": to * 2 + core}, device_id_type=MESH)
        copy.start()
        chip_sends.append(copy)
    for r in range(1, CHIPS):
        other_chip = lax.rem(chip + r, CHIPS)
        piece = r2.at[other_chip]
        pltpu.make_async_remote_copy(piece, piece, send_sem.at[0], r2_sem.at[other_chip], device_id=sibling,
                                     device_id_type=MESH).wait_recv()
    total = r2[0]
    for k in range(1, CHIPS):
        total += r2[k]
    half_out = halves.at[2 + core]
    halves[2 + core] = total * act[pl.ds(pl.multiple_of(rows * core, rows), rows), :]
    send(half_out, half_out, ("out",), sibling)
    arrive(halves.at[2 + other], ("out",))
    out[pl.ds(0, rows), :] = halves[2]
    out[pl.ds(rows, rows), :] = halves[3]

    for copy in sends + chip_sends:
        copy.wait_send()
    for b, copy in layer_sends:
        @pl.when(b != layer)
        def _():
            copy.wait_send()
    assert len(sends) <= N_SEND - 32 and len(keys) <= N_RECV, (len(sends), len(keys))


def shards(grads, decoder, active_ids, act_vals):
    pairs, _, rows, width = grads.shape
    n_feats = decoder.shape[2]
    tokens, slots = active_ids.shape
    keep = act_vals.shape[0]
    any_spec = pl.BlockSpec(memory_space=pl.ANY)
    return pl.pallas_call(
        kernel,
        name="edges",
        out_shape=jax.ShapeDtypeStruct((keep, slots), F32),
        in_specs=[any_spec] * 4,
        out_specs=pl.BlockSpec(memory_space=pltpu.VMEM),
        scratch_shapes=[
            pltpu.VMEM((2 * CHIPS, rows, width), jnp.bfloat16),
            pltpu.VMEM((2, n_feats, width), jnp.bfloat16),
            pltpu.VMEM((CHIPS, 2 * rows, 256), F32),
            pltpu.VMEM((tokens, slots), jnp.int32),
            pltpu.VMEM((keep, slots), F32),
            pltpu.VMEM((CHIPS, 2 * rows, slots), F32),
            pltpu.VMEM((LAYERS, keep, slots), F32),
            pltpu.VMEM((rows, slots), F32),
            pltpu.VMEM((CHIPS, rows, slots), F32),
            pltpu.VMEM((4, rows, slots), F32),
            pltpu.SemaphoreType.DMA((N_SEND,)),
            pltpu.SemaphoreType.DMA((N_RECV,)),
            pltpu.SemaphoreType.DMA((LAYERS,)),
            pltpu.SemaphoreType.DMA((CHIPS,)),
            pltpu.SemaphoreType.DMA((4,)),
        ],
        compiler_params=pltpu.CompilerParams(collective_id=0, has_side_effects=True, vmem_limit_bytes=48 << 20),
        cost_estimate=pl.CostEstimate(flops=2 * tokens * 2 * n_feats * width, bytes_accessed=4 << 20, transcendentals=0),
    )(grads, decoder, active_ids, act_vals)


def solution(mesh):
    placed = (P(None, "layer", "feat", None), P(None, "layer", "feat", None), P(), P("layer", None))
    return jax.shard_map(
        shards, mesh=mesh, in_specs=placed, out_specs=P("layer", None), check_vma=False
    )
```

```python
import jax
import jax.numpy as jnp
from jax import lax
from jax.experimental import pallas as pl
from jax.experimental.pallas import tpu as pltpu
from jax.sharding import PartitionSpec as P

MESH = pl.DeviceIdType.MESH
F32 = jnp.float32

RING = 8
CHIPS = 16
LAYERS = 16
END = 2560
PARTS = 2


def kernel(grads, dec, ids_hbm, act_hbm, out, got, feats, feats2, acc, acc2, ids, act, picked, r1, r2, half_out,
           send_sem, y_sem, x_sem, pair_sem, dec_sem, r1_sem, r2_sem, out_sem, loc_sem):
    layer = lax.axis_index("layer")
    feat = lax.axis_index("feat")
    core = lax.rem(feat, 2)
    chip = feat // 2
    row = lax.rem(chip, RING)
    side = chip // RING
    other = 1 - core
    rows = grads.shape[2]
    n_feats = dec.shape[2]
    kept = got.shape[2]
    width = kept // PARTS
    shared = kept - END

    def chip_at(which, off):
        base = side if which == 0 else 1 - side
        return base * RING + lax.rem(row + off + RING, RING)

    def device(which, off, c):
        return {"feat": chip_at(which, off) * 2 + c}

    def cols_of(of_side, p=None):
        lo = of_side * END
        if p is None:
            return pl.ds(pl.multiple_of(lo, 128), kept)
        return pl.ds(pl.multiple_of(lo + p * width, 128), width)

    def end_of(of_side):
        return pl.ds(pl.multiple_of(of_side * (END + shared), 128), END)

    sibling = device(0, 0, other)

    local = [
        pltpu.make_async_copy(grads.at[core, 0, :, cols_of(side)], got.at[feat], loc_sem.at[0]),
        pltpu.make_async_copy(dec.at[core, 0, :, cols_of(side)], feats.at[core], loc_sem.at[1]),
        pltpu.make_async_copy(ids_hbm, ids, loc_sem.at[2]),
        pltpu.make_async_copy(act_hbm, act, loc_sem.at[3]),
    ]

    barrier = pltpu.get_barrier_semaphore()
    peers = [device(0, s, c) for s in (1, -1) for c in (core, other)]
    peers += [device(1, 0, core), device(1, 0, other), sibling]
    for r in range(1, LAYERS):
        peers += [{"layer": lax.rem(layer + r, LAYERS), "feat": chip * 2 + c} for c in (core, other)]
    for peer in peers:
        pl.semaphore_signal(barrier, inc=1, device_id=peer, device_id_type=MESH)
    for copy in local:
        copy.start()
    pl.semaphore_wait(barrier, len(peers))

    def remote(src, dst, sem, to, out_at=0):
        return pltpu.make_async_remote_copy(src, dst, send_sem.at[out_at], sem, device_id=to, device_id_type=MESH)

    def send(src, dst, sem, to, out_at=0):
        remote(src, dst, sem, to, out_at).start()

    def sent(as_much_as, out_at):
        remote(as_much_as, as_much_as, send_sem.at[out_at], sibling, out_at).wait_send()

    def arrive(dst, sem):
        pltpu.make_async_remote_copy(dst, dst, send_sem.at[0], sem, device_id=sibling, device_id_type=MESH).wait_recv()

    def piece_of(b, p):
        return got.at[pl.ds(2 * b, 2), :, pl.ds(p * width, width)]

    def y_at(back, which, d, p):
        steps = 3 * PARTS + PARTS // 2
        return y_sem.at[back, which * steps + d * PARTS + (p if d < 3 else p % (PARTS // 2))]

    for p in range(PARTS):
        dst = got.at[feat, :, pl.ds(p * width, width)]
        for c in (core, other):
            for back, s in ((0, 1), (1, -1)):
                send(grads.at[c, 0, :, cols_of(side, p)], dst, y_at(back, 0, 0, p), device(0, s, c))
            send(grads.at[c, 0, :, cols_of(1 - side, p)], dst, x_sem.at[p], device(1, 0, c))
    send(grads.at[other, 0, :, cols_of(side)], got.at[feat], pair_sem.at[0], sibling)
    send(dec.at[other, 0, :, cols_of(side)], feats.at[core], pair_sem.at[1], sibling, 1)
    for c in (core, other):
        send(dec.at[c, 0, :, end_of(1 - side)], feats2.at[core], dec_sem.at[core], device(1, 0, c), 2)

    def joins(p):
        piece = piece_of(chip_at(1, 0), p)
        arrive(piece, x_sem.at[p])
        for back, s in ((0, 1), (1, -1)):
            send(piece, piece, y_at(back, 1, 0, p), device(0, s, core))

    def pass_on(which, d, p):
        for back, s in ((0, 1), (1, -1)):
            q = p if back == 0 or d == 0 else PARTS - 1 - p
            if d == 3 and p >= PARTS // 2:
                continue
            piece = piece_of(chip_at(which, -s * (d + 1)), q)
            arrive(piece, y_at(back, which, d, q))
            if d < 2 or (d == 2 and p < PARTS // 2):
                send(piece, piece, y_at(back, which, d + 1, q), device(0, s, core))

    def multiply(blocks):
        chips = [chip_at(which, off) for which, off in blocks]
        left = jnp.concatenate([got[pl.ds(2 * b, 2)].reshape(2 * rows, kept) for b in chips], axis=0)
        right = feats[...].reshape(2 * n_feats, kept)
        part = lax.dot_general(left, right, (((1,), (1,)), ((), ())), preferred_element_type=F32)
        for k, b in enumerate(chips):
            acc[b, :, pl.ds(0, 2 * n_feats)] = part[2 * rows * k: 2 * rows * (k + 1)]

    def multiply2(blocks):
        cols = pl.ds(pl.multiple_of(side * shared, 128), END)
        chips = [chip_at(which, off) for which, off in blocks]
        left = jnp.concatenate([got[pl.ds(2 * b, 2), :, cols].reshape(2 * rows, END) for b in chips], axis=0)
        right = feats2[...].reshape(2 * n_feats, END)
        part = lax.dot_general(left, right, (((1,), (1,)), ((), ())), preferred_element_type=F32)
        for k, b in enumerate(chips):
            acc2[b, :, pl.ds(0, 2 * n_feats)] = part[2 * rows * k: 2 * rows * (k + 1)]

    def pick(table, b, here):
        lanes = jnp.bitwise_and(here, 127)
        low = jnp.take_along_axis(table[b, :, pl.ds(0, 128)], lanes, axis=1, mode="promise_in_bounds")
        high = jnp.take_along_axis(table[b, :, pl.ds(128, 128)], lanes, axis=1, mode="promise_in_bounds")
        inside = jnp.logical_and(here >= 0, here < 2 * n_feats)
        return jnp.where(inside, jnp.where(here < 128, low, high), F32(0.0))

    def finish(blocks):
        for which, off in blocks:
            b = chip_at(which, off)
            named = ids[pl.ds(pl.multiple_of(2 * rows * b, 2 * rows), 2 * rows), :]
            value = pick(acc, b, named - chip * (2 * n_feats)) + pick(acc2, b, named - chip_at(1, 0) * (2 * n_feats))
            picked[b, 0] = value[:rows]
            picked[b, 1] = value[rows:]
            away = b != layer
            for c in (other, core):
                copy = remote(picked.at[b, c], r1.at[layer * 2 + core], r1_sem.at[0], {"layer": b, "feat": chip * 2 + c}, 3)
                if c is other:
                    copy.start()
                else:
                    pl.when(away)(copy.start)

    acc[...] = jnp.zeros_like(acc)
    acc2[...] = jnp.zeros_like(acc2)
    near = [(0, 0), (1, 0), (0, 1), (0, -1), (1, 1), (1, -1)]
    two = [(0, 2), (0, -2), (1, 2), (1, -2)]
    three = [(0, 3), (0, -3), (1, 3), (1, -3)]
    four = [(0, 4), (1, 4)]

    def step(which, d):
        for p in range(PARTS):
            pass_on(which, d, p)

    step(0, 0)
    for p in range(PARTS):
        joins(p)
    for copy in local:
        copy.wait()
    arrive(got.at[chip * 2 + other], pair_sem.at[0])
    arrive(feats.at[other], pair_sem.at[1])
    step(0, 1)
    step(1, 0)
    multiply(near)
    step(0, 2)
    step(1, 1)
    multiply(two)
    step(0, 3)
    step(1, 2)
    multiply(three)
    for c in (core, other):
        arrive(feats2.at[c], dec_sem.at[c])
    for blocks in (near, two, three):
        multiply2(blocks)
        finish(blocks)
    step(1, 3)
    multiply(four)
    multiply2(four)
    finish(four)

    r1[layer * 2 + core] = picked[layer, core]
    from_layers = r1.at[pl.ds(0, 2 * LAYERS - 1)]
    arrive(from_layers, r1_sem.at[0])
    total = r1[0]
    for k in range(1, 2 * LAYERS):
        total += r1[k]
    r2[chip] = total
    far_first = sorted([(which, off) for which in (0, 1) for off in range(RING) if (which, off) != (0, 0)],
                       key=lambda m: -(2 * m[0] + min(m[1], RING - m[1])))
    for which, off in far_first:
        send(r2.at[chip], r2.at[chip], r2_sem.at[0], device(which, off, core), 4)
    from_chips = r2.at[pl.ds(0, CHIPS - 1)]
    arrive(from_chips, r2_sem.at[0])
    total = r2[0]
    for k in range(1, CHIPS):
        total += r2[k]
    half_out[...] = total * act[pl.ds(pl.multiple_of(rows * core, rows), rows), :]
    to_out = out.at[pl.ds(pl.multiple_of(rows * core, rows), rows), :]
    send(half_out, to_out, out_sem.at[0], sibling, 5)
    own_out = pltpu.make_async_copy(half_out, to_out, loc_sem.at[4])
    own_out.start()

    sent(got.at[pl.ds(0, 31)], 0)
    sent(feats.at[0], 1)
    sent(feats2, 2)
    sent(from_layers, 3)
    sent(from_chips, 4)
    sent(half_out, 5)
    own_out.wait()
    arrive(out.at[pl.ds(pl.multiple_of(rows * other, rows), rows), :], out_sem.at[0])


def shards(grads, decoder, active_ids, act_vals):
    pairs, _, rows, width = grads.shape
    n_feats = decoder.shape[2]
    tokens, slots = active_ids.shape
    keep = act_vals.shape[0]
    kept = width - END
    any_spec = pl.BlockSpec(memory_space=pl.ANY)
    return pl.pallas_call(
        kernel,
        name="edges",
        out_shape=jax.ShapeDtypeStruct((keep, slots), F32),
        in_specs=[any_spec] * 4,
        out_specs=any_spec,
        scratch_shapes=[
            pltpu.VMEM((2 * CHIPS, rows, kept), jnp.bfloat16),
            pltpu.VMEM((2, n_feats, kept), jnp.bfloat16),
            pltpu.VMEM((2, n_feats, END), jnp.bfloat16),
            pltpu.VMEM((CHIPS, 2 * rows, 256), F32),
            pltpu.VMEM((CHIPS, 2 * rows, 256), F32),
            pltpu.VMEM((tokens, slots), jnp.int32),
            pltpu.VMEM((keep, slots), F32),
            pltpu.VMEM((CHIPS, 2, rows, slots), F32),
            pltpu.VMEM((2 * LAYERS, rows, slots), F32),
            pltpu.VMEM((CHIPS, rows, slots), F32),
            pltpu.VMEM((rows, slots), F32),
            pltpu.SemaphoreType.DMA((6,)),
            pltpu.SemaphoreType.DMA((2, 7 * PARTS)),
            pltpu.SemaphoreType.DMA((PARTS,)),
            pltpu.SemaphoreType.DMA((2,)),
            pltpu.SemaphoreType.DMA((2,)),
            pltpu.SemaphoreType.DMA((1,)),
            pltpu.SemaphoreType.DMA((1,)),
            pltpu.SemaphoreType.DMA((1,)),
            pltpu.SemaphoreType.DMA((5,)),
        ],
        compiler_params=pltpu.CompilerParams(collective_id=0, has_side_effects=True, vmem_limit_bytes=60 << 20),
        cost_estimate=pl.CostEstimate(flops=2 * tokens * 2 * n_feats * width, bytes_accessed=4 << 20, transcendentals=0),
    )(grads, decoder, active_ids, act_vals)


def solution(mesh):
    placed = (P(None, "layer", "feat", None), P(None, "layer", "feat", None), P(), P("layer", None))
    return jax.shard_map(
        shards, mesh=mesh, in_specs=placed, out_specs=P("layer", None), check_vma=False
    )
```

```python
import jax
import jax.numpy as jnp
from jax import lax
from jax.experimental import pallas as pl
from jax.experimental.pallas import tpu as pltpu
from jax.sharding import PartitionSpec as P

MESH = pl.DeviceIdType.MESH
F32 = jnp.float32

RING = 8
CHIPS = 16
LAYERS = 16
END = 2816
CHUNKS = ((0, 2304), (2304, 512))
PARTS = 2
VMEM_LIMIT = 55193 << 10


def kernel(grads, dec, ids_hbm, out, own, got, feats, feats2, acc, acc2, ids, picked, r1, r2, whole,
           send_sem, y_sem, x_sem, pair_sem, dec_sem, r1_sem, r2_sem, loc_sem):
    layer = lax.axis_index("layer")
    feat = lax.axis_index("feat")
    core = lax.rem(feat, 2)
    chip = feat // 2
    row = lax.rem(chip, RING)
    side = chip // RING
    other = 1 - core
    rows = grads.shape[2]
    n_feats = dec.shape[2]
    kept = got.shape[2]
    width = kept // PARTS
    shared = kept - END

    def chip_at(which, off):
        base = side if which == 0 else 1 - side
        return base * RING + lax.rem(row + off + RING, RING)

    def device(which, off, c):
        return {"feat": chip_at(which, off) * 2 + c}

    def cols_of(of_side, p=None):
        lo = of_side * END
        if p is None:
            return pl.ds(pl.multiple_of(lo, 128), kept)
        return pl.ds(pl.multiple_of(lo + p * width, 128), width)

    sibling = device(0, 0, other)

    local = [
        pltpu.make_async_copy(grads.at[core, 0, :, cols_of(side)], got.at[feat], loc_sem.at[0]),
        pltpu.make_async_copy(dec.at[core, 0, :, cols_of(side)], feats.at[core], loc_sem.at[1]),
        pltpu.make_async_copy(ids_hbm, ids, loc_sem.at[2]),
    ]
    own_rows = pltpu.make_async_copy(grads.at[:, 0], own, loc_sem.at[5])

    barrier = pltpu.get_barrier_semaphore()
    peers = [device(0, s, c) for s in (1, -1) for c in (core, other)]
    peers += [device(1, 0, core), device(1, 0, other), sibling]
    for r in range(1, LAYERS):
        peers += [{"layer": lax.rem(layer + r, LAYERS), "feat": chip * 2 + c} for c in (core, other)]
    for peer in peers:
        pl.semaphore_signal(barrier, inc=1, device_id=peer, device_id_type=MESH)
    own_rows.start()
    for copy in local:
        copy.start()
    pl.semaphore_wait(barrier, len(peers))
    own_rows.wait()

    def remote(src, dst, sem, to, out_at=0):
        return pltpu.make_async_remote_copy(src, dst, send_sem.at[out_at], sem, device_id=to, device_id_type=MESH)

    def send(src, dst, sem, to, out_at=0):
        remote(src, dst, sem, to, out_at).start()

    def sent(as_much_as, out_at):
        remote(as_much_as, as_much_as, send_sem.at[out_at], sibling, out_at).wait_send()

    def arrive(dst, sem):
        pltpu.make_async_remote_copy(dst, dst, send_sem.at[0], sem, device_id=sibling, device_id_type=MESH).wait_recv()

    def piece_of(b, p):
        return got.at[pl.ds(2 * b, 2), :, pl.ds(p * width, width)]

    def y_at(back, which, d, p):
        steps = 3 * PARTS + PARTS // 2
        return y_sem.at[back, which * steps + d * PARTS + (p if d < 3 else p % (PARTS // 2))]

    for p in range(PARTS):
        dst = got.at[feat, :, pl.ds(p * width, width)]
        for c in (core, other):
            for back, s in ((0, 1), (1, -1)):
                send(own.at[c, :, cols_of(side, p)], dst, y_at(back, 0, 0, p), device(0, s, c))
            send(own.at[c, :, cols_of(1 - side, p)], dst, x_sem.at[p], device(1, 0, c))
    send(own.at[other, :, cols_of(side)], got.at[feat], pair_sem.at[0], sibling)
    send(dec.at[other, 0, :, cols_of(side)], feats.at[core], pair_sem.at[1], sibling, 1)
    for k, (lo, size) in enumerate(CHUNKS):
        for c in (core, other):
            theirs = pl.ds(pl.multiple_of((1 - side) * (END + shared) + lo, 128), size)
            send(dec.at[c, 0, :, theirs], feats2.at[core, :, pl.ds(lo, size)], dec_sem.at[k], device(1, 0, c), 2)

    def joins(p):
        piece = piece_of(chip_at(1, 0), p)
        arrive(piece, x_sem.at[p])
        for back, s in ((0, 1), (1, -1)):
            send(piece, piece, y_at(back, 1, 0, p), device(0, s, core))

    def pass_on(which, d, p):
        for back, s in ((0, 1), (1, -1)):
            q = p if back == 0 or d == 0 else PARTS - 1 - p
            if d == 3 and p >= PARTS // 2:
                continue
            piece = piece_of(chip_at(which, -s * (d + 1)), q)
            arrive(piece, y_at(back, which, d, q))
            if d < 2 or (d == 2 and p < PARTS // 2):
                send(piece, piece, y_at(back, which, d + 1, q), device(0, s, core))

    def multiply(blocks):
        chips = [chip_at(which, off) for which, off in blocks]
        left = jnp.concatenate([got[pl.ds(2 * b, 2)].reshape(2 * rows, kept) for b in chips], axis=0)
        right = feats[...].reshape(2 * n_feats, kept)
        part = lax.dot_general(left, right, (((1,), (1,)), ((), ())), preferred_element_type=F32)
        for k, b in enumerate(chips):
            acc[b, :, pl.ds(0, 2 * n_feats)] = part[2 * rows * k: 2 * rows * (k + 1)]

    def multiply2(blocks, k):
        lo, size = CHUNKS[k]
        cols = pl.ds(pl.multiple_of(side * shared + lo, 128), size)
        chips = [chip_at(which, off) for which, off in blocks]
        left = jnp.concatenate([got[pl.ds(2 * b, 2), :, cols].reshape(2 * rows, size) for b in chips], axis=0)
        right = feats2[:, :, pl.ds(lo, size)].reshape(2 * n_feats, size)
        part = lax.dot_general(left, right, (((1,), (1,)), ((), ())), preferred_element_type=F32)
        for i, b in enumerate(chips):
            term = part[2 * rows * i: 2 * rows * (i + 1)]
            if k == 0:
                acc2[b, :, pl.ds(0, 2 * n_feats)] = term
            else:
                acc2[b, :, pl.ds(0, 2 * n_feats)] += term

    def end_rows(k):
        lo, size = CHUNKS[k]
        arrive(feats2.at[:, :, pl.ds(lo, size)], dec_sem.at[k])

    def pick(table, b, here):
        lanes = jnp.bitwise_and(here, 127)
        low = jnp.take_along_axis(table[b, :, pl.ds(0, 128)], lanes, axis=1, mode="promise_in_bounds")
        high = jnp.take_along_axis(table[b, :, pl.ds(128, 128)], lanes, axis=1, mode="promise_in_bounds")
        inside = jnp.logical_and(here >= 0, here < 2 * n_feats)
        return jnp.where(inside, jnp.where(here < 128, low, high), F32(0.0))

    def finish(blocks):
        for which, off in blocks:
            b = chip_at(which, off)
            named = ids[pl.ds(pl.multiple_of(2 * rows * b, 2 * rows), 2 * rows), :]
            value = pick(acc, b, named - chip * (2 * n_feats)) + pick(acc2, b, named - chip_at(1, 0) * (2 * n_feats))
            picked[b, 0] = value[:rows]
            picked[b, 1] = value[rows:]
            away = b != layer
            for c in (other, core):
                copy = remote(picked.at[b, c], r1.at[layer * 2 + core], r1_sem.at[0], {"layer": b, "feat": chip * 2 + c}, 3)
                if c is other:
                    copy.start()
                else:
                    pl.when(away)(copy.start)

    acc[...] = jnp.zeros_like(acc)
    acc2[...] = jnp.zeros_like(acc2)
    near = [(0, 0), (1, 0), (0, 1), (0, -1), (1, 1), (1, -1)]
    two = [(0, 2), (0, -2), (1, 2), (1, -2)]
    three = [(0, 3), (0, -3), (1, 3), (1, -3)]
    four = [(0, 4), (1, 4)]

    def step(which, d):
        for p in range(PARTS):
            pass_on(which, d, p)

    step(0, 0)
    for p in range(PARTS):
        joins(p)
    for copy in local:
        copy.wait()
    arrive(got.at[chip * 2 + other], pair_sem.at[0])
    arrive(feats.at[other], pair_sem.at[1])
    step(0, 1)
    step(1, 0)
    multiply(near)
    step(0, 2)
    step(1, 1)
    multiply(two)
    step(0, 3)
    step(1, 2)
    end_rows(0)
    multiply2(near + two, 0)
    multiply(three)
    multiply2(three, 0)
    end_rows(1)
    multiply2(near + two + three, 1)
    finish(near + two + three)
    step(1, 3)
    multiply(four)
    multiply2(four, 0)
    multiply2(four, 1)
    finish(four)

    r1[layer * 2 + core] = picked[layer, core]
    from_layers = r1.at[pl.ds(0, 2 * LAYERS - 1)]
    arrive(from_layers, r1_sem.at[0])
    total = r1[0]
    for k in range(1, 2 * LAYERS):
        total += r1[k]
    mine = chip * 2 + core
    r2[mine] = total
    far_first = sorted([(which, off) for which in (0, 1) for off in range(RING)],
                       key=lambda m: -(2 * m[0] + min(m[1], RING - m[1])))
    for which, off in far_first:
        for c in (other, core):
            if (which, off) != (0, 0) or c is other:
                send(r2.at[mine], r2.at[mine], r2_sem.at[0], device(which, off, c), 4)
    from_chips = r2.at[pl.ds(0, 2 * CHIPS - 1)]
    arrive(from_chips, r2_sem.at[0])
    for c in (0, 1):
        total = r2[c]
        for k in range(1, CHIPS):
            total += r2[2 * k + c]
        whole[pl.ds(rows * c, rows), :] = total
    own_out = pltpu.make_async_copy(whole, out, loc_sem.at[4])
    own_out.start()

    sent(got.at[pl.ds(0, 31)], 0)
    sent(feats.at[0], 1)
    sent(feats2, 2)
    sent(from_layers, 3)
    sent(from_chips, 4)
    own_out.wait()


def shards(grads, decoder, active_ids, act_vals):
    pairs, _, rows, width = grads.shape
    n_feats = decoder.shape[2]
    tokens, slots = active_ids.shape
    keep = act_vals.shape[0]
    kept = width - END
    any_spec = pl.BlockSpec(memory_space=pl.ANY)
    return pl.pallas_call(
        kernel,
        name="edges",
        out_shape=jax.ShapeDtypeStruct((keep, slots), F32),
        in_specs=[any_spec] * 3,
        out_specs=any_spec,
        scratch_shapes=[
            pltpu.VMEM((pairs, rows, width), jnp.bfloat16),
            pltpu.VMEM((2 * CHIPS, rows, kept), jnp.bfloat16),
            pltpu.VMEM((2, n_feats, kept), jnp.bfloat16),
            pltpu.VMEM((2, n_feats, END), jnp.bfloat16),
            pltpu.VMEM((CHIPS, 2 * rows, 256), F32),
            pltpu.VMEM((CHIPS, 2 * rows, 256), F32),
            pltpu.VMEM((tokens, slots), jnp.int32),
            pltpu.VMEM((CHIPS, 2, rows, slots), F32),
            pltpu.VMEM((2 * LAYERS, rows, slots), F32),
            pltpu.VMEM((2 * CHIPS, rows, slots), F32),
            pltpu.VMEM((keep, slots), F32),
            pltpu.SemaphoreType.DMA((6,)),
            pltpu.SemaphoreType.DMA((2, 7 * PARTS)),
            pltpu.SemaphoreType.DMA((PARTS,)),
            pltpu.SemaphoreType.DMA((2,)),
            pltpu.SemaphoreType.DMA((2,)),
            pltpu.SemaphoreType.DMA((1,)),
            pltpu.SemaphoreType.DMA((1,)),
            pltpu.SemaphoreType.DMA((6,)),
        ],
        compiler_params=pltpu.CompilerParams(collective_id=0, has_side_effects=True, vmem_limit_bytes=VMEM_LIMIT),
        cost_estimate=pl.CostEstimate(flops=2 * tokens * 2 * n_feats * width, bytes_accessed=4 << 20, transcendentals=0),
    )(grads, decoder, active_ids) * act_vals


def solution(mesh):
    placed = (P(None, "layer", "feat", None), P(None, "layer", "feat", None), P(), P("layer", None))
    return jax.shard_map(
        shards, mesh=mesh, in_specs=placed, out_specs=P("layer", None), check_vma=False
    )
```

```python
import jax
import jax.numpy as jnp
from jax import lax
from jax.experimental import pallas as pl
from jax.experimental.pallas import tpu as pltpu
from jax.sharding import PartitionSpec as P

MESH = pl.DeviceIdType.MESH
F32 = jnp.float32

RING = 8
CHIPS = 16
LAYERS = 16
END = 2816
CHUNKS = ((0, 2304), (2304, 512))
PARTS = 2
VMEM_LIMIT = 55193 << 10


def kernel(grads, dec, ids_hbm, out, own, got, feats, feats2, acc, acc2, ids, picked, from_pair, both, r1, r2, whole,
           send_sem, y_sem, x_sem, pair_sem, dec_sem, r1_sem, r2_sem, half_sem, loc_sem):
    layer = lax.axis_index("layer")
    feat = lax.axis_index("feat")
    core = lax.rem(feat, 2)
    chip = feat // 2
    row = lax.rem(chip, RING)
    side = chip // RING
    other = 1 - core
    rows = grads.shape[2]
    n_feats = dec.shape[2]
    kept = got.shape[2]
    width = kept // PARTS
    shared = kept - END

    def chip_at(which, off):
        base = side if which == 0 else 1 - side
        return base * RING + lax.rem(row + off + RING, RING)

    def device(which, off, c):
        return {"feat": chip_at(which, off) * 2 + c}

    def cols_of(of_side, p=None):
        lo = of_side * END
        if p is None:
            return pl.ds(pl.multiple_of(lo, 128), kept)
        return pl.ds(pl.multiple_of(lo + p * width, 128), width)

    sibling = device(0, 0, other)

    local = [
        pltpu.make_async_copy(grads.at[core, 0, :, cols_of(side)], got.at[feat], loc_sem.at[0]),
        pltpu.make_async_copy(dec.at[core, 0, :, cols_of(side)], feats.at[core], loc_sem.at[1]),
        pltpu.make_async_copy(ids_hbm, ids, loc_sem.at[2]),
    ]
    own_rows = pltpu.make_async_copy(grads.at[:, 0], own, loc_sem.at[5])

    barrier = pltpu.get_barrier_semaphore()
    peers = [device(0, s, c) for s in (1, -1) for c in (core, other)]
    peers += [device(1, 0, core), device(1, 0, other), sibling]
    peers += [{"layer": lax.rem(layer + r, LAYERS)} for r in range(1, LAYERS)]
    for peer in peers:
        pl.semaphore_signal(barrier, inc=1, device_id=peer, device_id_type=MESH)
    own_rows.start()
    for copy in local:
        copy.start()
    pl.semaphore_wait(barrier, len(peers))
    own_rows.wait()

    def remote(src, dst, sem, to, out_at=0):
        return pltpu.make_async_remote_copy(src, dst, send_sem.at[out_at], sem, device_id=to, device_id_type=MESH)

    def send(src, dst, sem, to, out_at=0):
        remote(src, dst, sem, to, out_at).start()

    def sent(as_much_as, out_at):
        remote(as_much_as, as_much_as, send_sem.at[out_at], sibling, out_at).wait_send()

    def arrive(dst, sem):
        pltpu.make_async_remote_copy(dst, dst, send_sem.at[0], sem, device_id=sibling, device_id_type=MESH).wait_recv()

    def piece_of(b, p):
        return got.at[pl.ds(2 * b, 2), :, pl.ds(p * width, width)]

    def y_at(back, which, d, p):
        steps = 3 * PARTS + PARTS // 2
        return y_sem.at[back, which * steps + d * PARTS + (p if d < 3 else p % (PARTS // 2))]

    for p in range(PARTS):
        dst = got.at[feat, :, pl.ds(p * width, width)]
        for c in (core, other):
            for back, s in ((0, 1), (1, -1)):
                send(own.at[c, :, cols_of(side, p)], dst, y_at(back, 0, 0, p), device(0, s, c))
            send(own.at[c, :, cols_of(1 - side, p)], dst, x_sem.at[p], device(1, 0, c))
    send(own.at[other, :, cols_of(side)], got.at[feat], pair_sem.at[0], sibling)
    send(dec.at[other, 0, :, cols_of(side)], feats.at[core], pair_sem.at[1], sibling, 1)
    for k, (lo, size) in enumerate(CHUNKS):
        for c in (core, other):
            theirs = pl.ds(pl.multiple_of((1 - side) * (END + shared) + lo, 128), size)
            send(dec.at[c, 0, :, theirs], feats2.at[core, :, pl.ds(lo, size)], dec_sem.at[k], device(1, 0, c), 2)

    def joins(p):
        piece = piece_of(chip_at(1, 0), p)
        arrive(piece, x_sem.at[p])
        for back, s in ((0, 1), (1, -1)):
            send(piece, piece, y_at(back, 1, 0, p), device(0, s, core))

    def pass_on(which, d, p):
        for back, s in ((0, 1), (1, -1)):
            q = p if back == 0 or d == 0 else PARTS - 1 - p
            if d == 3 and p >= PARTS // 2:
                continue
            piece = piece_of(chip_at(which, -s * (d + 1)), q)
            arrive(piece, y_at(back, which, d, q))
            if d < 2 or (d == 2 and p < PARTS // 2):
                send(piece, piece, y_at(back, which, d + 1, q), device(0, s, core))

    def multiply(blocks):
        chips = [chip_at(which, off) for which, off in blocks]
        left = jnp.concatenate([got[pl.ds(2 * b, 2)].reshape(2 * rows, kept) for b in chips], axis=0)
        right = feats[...].reshape(2 * n_feats, kept)
        part = lax.dot_general(left, right, (((1,), (1,)), ((), ())), preferred_element_type=F32)
        for k, b in enumerate(chips):
            acc[b, :, pl.ds(0, 2 * n_feats)] = part[2 * rows * k: 2 * rows * (k + 1)]

    def multiply2(blocks, k):
        lo, size = CHUNKS[k]
        cols = pl.ds(pl.multiple_of(side * shared + lo, 128), size)
        chips = [chip_at(which, off) for which, off in blocks]
        left = jnp.concatenate([got[pl.ds(2 * b, 2), :, cols].reshape(2 * rows, size) for b in chips], axis=0)
        right = feats2[:, :, pl.ds(lo, size)].reshape(2 * n_feats, size)
        part = lax.dot_general(left, right, (((1,), (1,)), ((), ())), preferred_element_type=F32)
        for i, b in enumerate(chips):
            term = part[2 * rows * i: 2 * rows * (i + 1)]
            if k == 0:
                acc2[b, :, pl.ds(0, 2 * n_feats)] = term
            else:
                acc2[b, :, pl.ds(0, 2 * n_feats)] += term

    def end_rows(k):
        lo, size = CHUNKS[k]
        arrive(feats2.at[:, :, pl.ds(lo, size)], dec_sem.at[k])

    def pick(table, b, here):
        lanes = jnp.bitwise_and(here, 127)
        low = jnp.take_along_axis(table[b, :, pl.ds(0, 128)], lanes, axis=1, mode="promise_in_bounds")
        high = jnp.take_along_axis(table[b, :, pl.ds(128, 128)], lanes, axis=1, mode="promise_in_bounds")
        inside = jnp.logical_and(here >= 0, here < 2 * n_feats)
        return jnp.where(inside, jnp.where(here < 128, low, high), F32(0.0))

    def choose(blocks, at):
        for k, (which, off) in enumerate(blocks):
            b = chip_at(which, off)
            named = ids[pl.ds(pl.multiple_of(2 * rows * b, 2 * rows), 2 * rows), :]
            value = pick(acc, b, named - chip * (2 * n_feats)) + pick(acc2, b, named - chip_at(1, 0) * (2 * n_feats))
            picked[0, at + k] = value[:rows]
            picked[1, at + k] = value[rows:]
        span = pl.ds(at, len(blocks))
        send(picked.at[other, span], from_pair.at[span], half_sem.at[0 if at == 0 else 1], sibling, 5)

    def finish(blocks, at):
        span = pl.ds(at, len(blocks))
        arrive(from_pair.at[span], half_sem.at[0 if at == 0 else 1])
        for k, (which, off) in enumerate(blocks):
            b = chip_at(which, off)
            both[at + k] = picked[core, at + k] + from_pair[at + k]
            copy = remote(both.at[at + k], r1.at[layer], r1_sem.at[0], {"layer": b}, 3)
            away = b != layer
            pl.when(away)(copy.start)

            @pl.when(jnp.logical_not(away))
            def _():
                r1[layer] = both[at + k]

    acc[...] = jnp.zeros_like(acc)
    acc2[...] = jnp.zeros_like(acc2)
    near = [(0, 0), (1, 0), (0, 1), (0, -1), (1, 1), (1, -1)]
    two = [(0, 2), (0, -2), (1, 2), (1, -2)]
    three = [(0, 3), (0, -3), (1, 3), (1, -3)]
    four = [(0, 4), (1, 4)]

    def step(which, d):
        for p in range(PARTS):
            pass_on(which, d, p)

    step(0, 0)
    for p in range(PARTS):
        joins(p)
    for copy in local:
        copy.wait()
    arrive(got.at[chip * 2 + other], pair_sem.at[0])
    arrive(feats.at[other], pair_sem.at[1])
    step(0, 1)
    step(1, 0)
    multiply(near)
    step(0, 2)
    step(1, 1)
    multiply(two)
    step(0, 3)
    step(1, 2)
    end_rows(0)
    multiply2(near + two, 0)
    multiply(three)
    multiply2(three, 0)
    early = near + two + three
    end_rows(1)
    multiply2(early, 1)
    choose(early, 0)
    step(1, 3)
    multiply(four)
    finish(early, 0)
    multiply2(four, 0)
    multiply2(four, 1)
    choose(four, len(early))
    finish(four, len(early))

    from_layers = r1.at[pl.ds(0, LAYERS - 1)]
    arrive(from_layers, r1_sem.at[0])
    total = r1[0]
    for k in range(1, LAYERS):
        total += r1[k]
    mine = chip * 2 + core
    r2[mine] = total
    far_first = sorted([(which, off) for which in (0, 1) for off in range(RING)],
                       key=lambda m: -(2 * m[0] + min(m[1], RING - m[1])))
    for which, off in far_first:
        for c in (other, core):
            if (which, off) != (0, 0) or c is other:
                send(r2.at[mine], r2.at[mine], r2_sem.at[0], device(which, off, c), 4)
    from_chips = r2.at[pl.ds(0, 2 * CHIPS - 1)]
    arrive(from_chips, r2_sem.at[0])
    for c in (0, 1):
        total = r2[c]
        for k in range(1, CHIPS):
            total += r2[2 * k + c]
        whole[pl.ds(rows * c, rows), :] = total
    own_out = pltpu.make_async_copy(whole, out, loc_sem.at[4])
    own_out.start()

    sent(got.at[pl.ds(0, 31)], 0)
    sent(feats.at[0], 1)
    sent(feats2, 2)
    sent(from_layers, 3)
    sent(from_chips, 4)
    sent(from_pair, 5)
    own_out.wait()


def shards(grads, decoder, active_ids, act_vals):
    pairs, _, rows, width = grads.shape
    n_feats = decoder.shape[2]
    tokens, slots = active_ids.shape
    keep = act_vals.shape[0]
    kept = width - END
    any_spec = pl.BlockSpec(memory_space=pl.ANY)
    return pl.pallas_call(
        kernel,
        name="edges",
        out_shape=jax.ShapeDtypeStruct((keep, slots), F32),
        in_specs=[any_spec] * 3,
        out_specs=any_spec,
        scratch_shapes=[
            pltpu.VMEM((pairs, rows, width), jnp.bfloat16),
            pltpu.VMEM((2 * CHIPS, rows, kept), jnp.bfloat16),
            pltpu.VMEM((2, n_feats, kept), jnp.bfloat16),
            pltpu.VMEM((2, n_feats, END), jnp.bfloat16),
            pltpu.VMEM((CHIPS, 2 * rows, 256), F32),
            pltpu.VMEM((CHIPS, 2 * rows, 256), F32),
            pltpu.VMEM((tokens, slots), jnp.int32),
            pltpu.VMEM((2, CHIPS, rows, slots), F32),
            pltpu.VMEM((CHIPS, rows, slots), F32),
            pltpu.VMEM((CHIPS, rows, slots), F32),
            pltpu.VMEM((LAYERS, rows, slots), F32),
            pltpu.VMEM((2 * CHIPS, rows, slots), F32),
            pltpu.VMEM((keep, slots), F32),
            pltpu.SemaphoreType.DMA((6,)),
            pltpu.SemaphoreType.DMA((2, 7 * PARTS)),
            pltpu.SemaphoreType.DMA((PARTS,)),
            pltpu.SemaphoreType.DMA((2,)),
            pltpu.SemaphoreType.DMA((2,)),
            pltpu.SemaphoreType.DMA((1,)),
            pltpu.SemaphoreType.DMA((1,)),
            pltpu.SemaphoreType.DMA((2,)),
            pltpu.SemaphoreType.DMA((6,)),
        ],
        compiler_params=pltpu.CompilerParams(collective_id=0, has_side_effects=True, vmem_limit_bytes=VMEM_LIMIT),
        cost_estimate=pl.CostEstimate(flops=2 * tokens * 2 * n_feats * width, bytes_accessed=4 << 20, transcendentals=0),
    )(grads, decoder, active_ids) * act_vals


def solution(mesh):
    placed = (P(None, "layer", "feat", None), P(None, "layer", "feat", None), P(), P("layer", None))
    return jax.shard_map(
        shards, mesh=mesh, in_specs=placed, out_specs=P("layer", None), check_vma=False
    )
```
